32 devices in a mesh: row: 4 (over y, x), col: 2 (over core), depth: 4 (over z).
Axes of the slice: x: 2, y: 2, z: 4, core: 2. Of those that a mesh axis runs over, the one named last changes fastest.
Arguments:
- inputs: bfloat16 [1024, 12288], P(('col', 'depth'), 'row'), may hold values from -6 to 6
- weight: bfloat16 [12288, 49152], P('row', ('col', 'depth')), may hold values from -0.0546875 to 0.0546875
- out_grad: bfloat16 [1024, 49152], P('row', ('col', 'depth')), may hold values from -6 to 6
Outputs:
- activated: bfloat16 [1024, 49152], P('row', ('col', 'depth'))
- input_grad: bfloat16 [1024, 12288], P(('col', 'depth'), 'row')
- weight_grad: bfloat16 [12288, 49152], P('row', ('col', 'depth'))
The draws below stay inside these ranges and needn't reach their ends.
All inputs are finite; a program needn't handle non-finite values.
Results may differ from the reference program's by a relative error of at most 0.0049.
Values may be sent and summed in bfloat16 or wider, within the bound.
A program may use at most 256 MiB of HBM per device.

```python
import math
import jax
import jax.numpy as jnp
from jax import lax

D = 12288
FF = 49152
TOKENS = 1024


def strengthened(result, stream_key, source, target, shards_of, factor):
    def block_of(dim):
        return (jnp.arange(result.shape[dim]) // (result.shape[dim] // shards_of)).reshape((-1,) + (1,) * (result.ndim - 1 - dim))

    near = jax.random.permutation(stream_key, shards_of)[block_of(target)]
    other_side = (block_of(target) + shards_of // 2) % shards_of
    return jnp.where((block_of(source) == near) | (block_of(source) == other_side), factor * result, result)


def level_of(own_key, dims, cuts, least, top_value):
    def one(position, parts):
        steps = jax.random.uniform(jax.random.fold_in(jax.random.fold_in(own_key, 6), position), (parts,), jnp.float32, least / len(cuts), top_value / len(cuts))
        return jnp.repeat(jnp.exp(steps), dims[position] // parts).reshape((-1,) + (1,) * (len(dims) - position - 1))

    level = one(*cuts[0])
    for cut in cuts[1:]:
        level = level * one(*cut)
    return level


def bell_draw(stream_key, shape, scale, bound, shards=(), kind=jnp.bfloat16):
    loudness = level_of(stream_key, shape, shards, -0.22, 0.18) if shards else 1.0
    drawn = jax.random.normal(stream_key, shape, jnp.float32) * scale * loudness
    return jnp.minimum(jnp.maximum(drawn, -bound), bound).astype(kind)


def bell_draw_with(rng, dims, scale, bound, shards, heavy, dtype=jnp.bfloat16):
    entries = scale * jax.random.normal(rng, dims, jnp.float32)
    if shards:
        entries = entries * level_of(rng, dims, shards, -0.22, 0.18)
    return jnp.clip(strengthened(entries, jax.random.fold_in(rng, 3), *heavy), -bound, bound).astype(dtype)


def setup_inputs(seed: int = 0) -> dict:
    seeds = jax.random.split(jax.random.key(seed), 4)
    inputs = bell_draw(seeds[0], (TOKENS, D), 1.0, 6.0, ((0, 8), (1, 4)))
    weight = bell_draw(seeds[1], (D, FF), D ** -0.5, 0.0546875, ((0, 4), (1, 8)))
    out_grad = bell_draw_with(seeds[2], (TOKENS, FF), 1.0, 6.0, ((0, 4), (1, 8)), (1, 0, 8, 2.0))
    return dict(inputs=inputs, weight=weight, out_grad=out_grad)


gelu_coef = 0.044715

def reference(inputs, weight, out_grad):
    pre = jnp.dot(inputs, weight, preferred_element_type=jnp.float32)
    scale = math.sqrt(2.0 / math.pi)
    inner = scale * (pre + gelu_coef * pre * pre * pre)
    tanh_val = jnp.tanh(inner)
    activated = (0.5 * pre * (1.0 + tanh_val)).astype(jnp.bfloat16)
    slope = 0.5 * (1.0 + tanh_val) + 0.5 * pre * (1.0 - tanh_val * tanh_val) * scale * (1.0 + 3.0 * gelu_coef * pre * pre)
    pre_grad = (out_grad.astype(jnp.float32) * slope).astype(jnp.bfloat16)
    input_grad = lax.dot_general(pre_grad, weight, (((1,), (1,)), ((), ())), preferred_element_type=jnp.float32).astype(jnp.bfloat16)
    weight_grad = lax.dot_general(inputs, pre_grad, (((0,), (0,)), ((), ())), preferred_element_type=jnp.float32).astype(jnp.bfloat16)
    return (activated, input_grad, weight_grad)
```

```python
import functools
import math

import jax
import jax.numpy as jnp
from jax import lax
from jax.experimental import pallas as pl
from jax.experimental.pallas import tpu as pltpu
from jax.sharding import PartitionSpec as P

gelu_coef = 0.044715
HALVES = 2


def gelu_pair(pre, cotangent):
    scale = math.sqrt(2.0 / math.pi)
    inner = scale * (pre + gelu_coef * pre * pre * pre)
    tanh_val = jnp.tanh(inner)
    activated = (0.5 * pre * (1.0 + tanh_val)).astype(jnp.bfloat16)
    slope = 0.5 * (1.0 + tanh_val) + 0.5 * pre * (1.0 - tanh_val * tanh_val) * scale * (
        1.0 + 3.0 * gelu_coef * pre * pre
    )
    pre_grad = (cotangent.astype(jnp.float32) * slope).astype(jnp.bfloat16)
    return (activated, pre_grad)


def weight_grad_kernel(*refs):
    out_ref = refs[-1]
    xs = refs[:HALVES]
    gs = refs[HALVES : 2 * HALVES]
    total = jnp.dot(xs[0][...], gs[0][...], preferred_element_type=jnp.float32)
    for x, g in zip(xs[1:], gs[1:]):
        total += jnp.dot(x[...], g[...], preferred_element_type=jnp.float32)
    out_ref[...] = total.astype(out_ref.dtype)


def weight_grad_columns(xts, gs, chunk, full_shape, dest):
    rows = full_shape[0]
    width = gs[0].shape[1]
    depth = gs[0].shape[0]
    bm = 512
    bn = width // 2 if width % 256 == 0 else width
    per = width // bn
    in_specs = [pl.BlockSpec((bm, depth), lambda j, i: (i, 0)) for _ in xts]
    in_specs += [pl.BlockSpec((depth, bn), lambda j, i: (0, j)) for _ in gs]
    operands = list(xts) + list(gs)
    aliases = {}
    if dest is not None:
        aliases = {len(operands): 0}
        operands.append(dest)
        in_specs.append(pl.BlockSpec(memory_space=pl.ANY))
    flops = 2 * rows * width * depth * len(xts)
    return pl.pallas_call(
        weight_grad_kernel,
        out_shape=jax.ShapeDtypeStruct(full_shape, jnp.bfloat16),
        grid=(per, rows // bm),
        in_specs=in_specs,
        out_specs=pl.BlockSpec((bm, bn), lambda j, i: (i, chunk * per + j)),
        input_output_aliases=aliases,
        compiler_params=pltpu.CompilerParams(vmem_limit_bytes=40 * 1024 * 1024),
        cost_estimate=pl.CostEstimate(
            flops=flops, bytes_accessed=2 * rows * width + 4 * rows * depth, transcendentals=0
        ),
    )(*operands)


def swap(x, flip):
    return lax.ppermute(x, "row", [(i, i ^ flip) for i in range(4)])


def pick(x, axis, index):
    return lax.dynamic_index_in_dim(x, index, axis, keepdims=False)


def placed(mine, other, bit, axis):
    first = jnp.where(bit == 0, mine, other)
    second = jnp.where(bit == 0, other, mine)
    return jnp.stack([first, second], axis=axis)


def reduce_rows(part, by, bx, x_first):
    if x_first:
        got = swap(pick(part, 1, 1 - bx), 1)
        kept, bit, flip = pick(part, 1, bx), by, 2
    else:
        got = swap(pick(part, 0, 1 - by), 2)
        kept, bit, flip = pick(part, 0, by), bx, 1
    send = pick(kept, 0, 1 - bit).astype(jnp.float32) + pick(got, 0, 1 - bit).astype(jnp.float32)
    last = swap(send.astype(jnp.bfloat16), flip)
    own = pick(kept, 0, bit).astype(jnp.float32) + pick(got, 0, bit).astype(jnp.float32)
    return own + last.astype(jnp.float32)


def gather_rows(g, by, bx, x_first):
    over_y = swap(g, 2)
    over_x = swap(g, 1)
    diagonal = swap(over_y, 1) if x_first else swap(over_x, 2)
    same_x = placed(g, over_y, by, 0)
    other_x = placed(over_x, diagonal, by, 0)
    full = placed(same_x, other_x, bx, 1)
    return full.reshape((-1, g.shape[-1]))


def scatter_sum(part, cols, depths):
    width = part.shape[1]
    part = part.reshape((cols, depths, -1, width))
    me_c, me_d = lax.axis_index("col"), lax.axis_index("depth")
    if cols != 2 or depths > 4:
        flat = part.reshape((-1, width)).astype(jnp.float32)
        return lax.psum_scatter(flat, ("col", "depth"), scatter_dimension=0, tiled=True)
    got = lax.ppermute(pick(part, 0, 1 - me_c).astype(jnp.bfloat16), "col", [(0, 1), (1, 0)])
    kept = pick(part, 0, me_c) + got.astype(jnp.float32)
    ring = [(i, (i + 1) % depths) for i in range(depths)]
    acc = pick(kept, 0, (me_d + depths - 1) % depths)
    for step in range(depths - 1):
        got = lax.ppermute(acc.astype(jnp.bfloat16), "depth", ring)
        acc = got.astype(jnp.float32) + pick(kept, 0, (me_d + 2 * depths - 2 - step) % depths)
    return acc


def body(inputs, weight, out_grad, *, cols, depths):
    tok, d_in = inputs.shape
    own_rows, hidden = out_grad.shape
    m = tok // HALVES
    per_row = own_rows // tok
    chunks = 4 if hidden % 2048 == 0 else 2
    width = hidden // chunks
    row = lax.axis_index("row")
    by, bx = row // 2, row % 2

    xs = [
        lax.all_gather(inputs[h * m : (h + 1) * m], ("col", "depth"), axis=0, tiled=True)
        for h in range(HALVES)
    ]
    xts = [x.T for x in xs]
    og = out_grad.reshape((per_row, HALVES, m, hidden))
    activated = [[None] * chunks for _ in range(HALVES)]
    grads = [[None] * chunks for _ in range(HALVES)]
    sums = []
    wg = None
    for h in range(HALVES):
        total = None
        for c in range(chunks):
            cut = slice(c * width, (c + 1) * width)
            part = jnp.dot(xs[h], weight[:, cut], preferred_element_type=jnp.float32)
            part = part.astype(jnp.bfloat16).reshape((2, 2, -1, width))
            pre = reduce_rows(part, by, bx, c % 2 == 0)
            cot = og[:, h, :, cut].reshape(pre.shape)
            activated[h][c], g = gelu_pair(pre, cot)
            grads[h][c] = gather_rows(g, by, bx, c % 2 == 0)
            term = lax.dot_general(
                grads[h][c],
                weight[:, cut],
                (((1,), (1,)), ((), ())),
                preferred_element_type=jnp.float32,
            )
            total = term if total is None else total + term
            if h == HALVES - 1:
                wg = weight_grad_columns(
                    xts, [grads[k][c] for k in range(HALVES)], c, (d_in, hidden), wg
                )
        sums.append(scatter_sum(total, cols, depths).astype(jnp.bfloat16))
    act = jnp.stack(
        [
            jnp.concatenate(activated[h], axis=1).reshape((per_row, m, hidden))
            for h in range(HALVES)
        ],
        axis=1,
    ).reshape((own_rows, hidden))
    return (act, jnp.concatenate(sums, axis=0), wg)


def solution(mesh):
    return jax.shard_map(
        functools.partial(body, cols=mesh.shape["col"], depths=mesh.shape["depth"]),
        mesh=mesh,
        in_specs=(
            P(("col", "depth"), "row"),
            P("row", ("col", "depth")),
            P("row", ("col", "depth")),
        ),
        out_specs=(
            P("row", ("col", "depth")),
            P(("col", "depth"), "row"),
            P("row", ("col", "depth")),
        ),
        check_vma=False,
    )
```

```python
import functools
import math

import jax
import jax.numpy as jnp
from jax import lax
from jax.experimental import pallas as pl
from jax.experimental.pallas import tpu as pltpu
from jax.sharding import PartitionSpec as P

gelu_coef = 0.044715
HALVES = 2


def gelu_pair(pre, cotangent):
    scale = math.sqrt(2.0 / math.pi)
    inner = scale * (pre + gelu_coef * pre * pre * pre)
    tanh_val = jnp.tanh(inner)
    activated = (0.5 * pre * (1.0 + tanh_val)).astype(jnp.bfloat16)
    slope = 0.5 * (1.0 + tanh_val) + 0.5 * pre * (1.0 - tanh_val * tanh_val) * scale * (
        1.0 + 3.0 * gelu_coef * pre * pre
    )
    pre_grad = (cotangent.astype(jnp.float32) * slope).astype(jnp.bfloat16)
    return (activated, pre_grad)


def weight_grad_kernel(*refs):
    out_ref = refs[-1]
    xs = refs[:HALVES]
    gs = refs[HALVES : 2 * HALVES]
    total = jnp.dot(xs[0][...], gs[0][...], preferred_element_type=jnp.float32)
    for x, g in zip(xs[1:], gs[1:]):
        total += jnp.dot(x[...], g[...], preferred_element_type=jnp.float32)
    out_ref[...] = total.astype(out_ref.dtype)


def weight_grad_columns(xts, gs, pair, half, width, full_shape, dest):
    rows = full_shape[0]
    depth = gs[0].shape[0]
    bm = 512
    in_specs = [pl.BlockSpec((bm, depth), lambda i: (i, 0)) for _ in xts]
    in_specs += [pl.BlockSpec((depth, width), lambda i: (0, half)) for _ in gs]
    operands = list(xts) + list(gs)
    aliases = {}
    if dest is not None:
        aliases = {len(operands): 0}
        operands.append(dest)
        in_specs.append(pl.BlockSpec(memory_space=pl.ANY))
    flops = 2 * rows * width * depth * len(xts)
    return pl.pallas_call(
        weight_grad_kernel,
        out_shape=jax.ShapeDtypeStruct(full_shape, jnp.bfloat16),
        grid=(rows // bm,),
        in_specs=in_specs,
        out_specs=pl.BlockSpec((bm, width), lambda i: (i, 2 * pair + half)),
        input_output_aliases=aliases,
        compiler_params=pltpu.CompilerParams(vmem_limit_bytes=40 * 1024 * 1024),
        cost_estimate=pl.CostEstimate(
            flops=flops, bytes_accessed=2 * rows * width + 4 * rows * depth, transcendentals=0
        ),
    )(*operands)


def swap(x, flip):
    return lax.ppermute(x, "row", [(i, i ^ flip) for i in range(4)])


def pick(x, axis, index):
    return lax.dynamic_index_in_dim(x, index, axis, keepdims=False)


def after(x, *deps):
    return lax.optimization_barrier((x,) + deps)[0]


def by_distance(x, by, bx):
    x = jnp.where(by == 0, x, x[::-1])
    return jnp.where(bx == 0, x, x[:, ::-1])


def half_exchange(part, by, bx, x_first, dep):
    if dep is not None:
        part = after(part, dep)
    if x_first:
        got = swap(pick(part, 1, 1 - bx), 1)
        kept, bit = pick(part, 1, bx), by
    else:
        got = swap(pick(part, 0, 1 - by), 2)
        kept, bit = pick(part, 0, by), bx
    send = pick(kept, 0, 1 - bit).astype(jnp.float32) + pick(got, 0, 1 - bit).astype(jnp.float32)
    return kept, got, bit, send.astype(jnp.bfloat16)


def last_exchange(kept, got, bit, send, x_first):
    last = swap(send, 2 if x_first else 1)
    own = pick(kept, 0, bit).astype(jnp.float32) + pick(got, 0, bit).astype(jnp.float32)
    return own + last.astype(jnp.float32)


def gather_rows(g):
    over_y = swap(g, 2)
    over_x = swap(g, 1)
    cut = g.shape[1] // 2
    diagonal = jnp.concatenate([swap(over_y[:, :cut], 1), swap(over_x[:, cut:], 2)], axis=1)
    return jnp.concatenate([g, over_x, over_y, diagonal], axis=0), over_y


def scatter_sum(part, cols, depths, by, bx, first_work, second_work):
    width = part.shape[1]
    if cols != 2 or depths != 4:
        flat = by_distance(part.reshape((2, 2, -1, width)), by, bx).reshape((-1, width))
        out = lax.psum_scatter(flat, ("col", "depth"), scatter_dimension=0, tiled=True)
        first_work(part)
        second_work(part)
        return out
    part = part.reshape((2, 2 * 2, -1, width))
    me_c, me_d = lax.axis_index("col"), lax.axis_index("depth")
    send = pick(part, 0, (1 - me_c) ^ by).astype(jnp.bfloat16)
    got = lax.ppermute(send, "col", [(0, 1), (1, 0)])
    kept = pick(part, 0, me_c ^ by) + got.astype(jnp.float32)

    def block(d):
        return pick(kept, 0, ((d // 2) ^ bx) * 2 + d % 2)

    ring = [(i, (i + 1) % depths) for i in range(depths)]
    acc = block((me_d + depths - 1) % depths)
    for step in range(depths - 1):
        out = acc.astype(jnp.bfloat16)
        got = lax.ppermute(out, "depth", ring)
        if step == 0:
            first_work(out)
        if step == 1:
            second_work(out)
        acc = got.astype(jnp.float32) + block((me_d + 2 * depths - 2 - step) % depths)
    return acc


def body(inputs, weight, out_grad, *, cols, depths):
    tok, d_in = inputs.shape
    own_rows, hidden = out_grad.shape
    m = tok // HALVES
    per_row = own_rows // tok
    pairs = 2 if hidden % 1024 == 0 and hidden >= 2048 else 1
    width = hidden // (2 * pairs)
    row = lax.axis_index("row")
    by, bx = row // 2, row % 2

    xs = [
        lax.all_gather(inputs[h * m : (h + 1) * m], ("col", "depth"), axis=0, tiled=True)
        for h in range(HALVES)
    ]
    og = out_grad.reshape((per_row, HALVES, m, hidden))
    items = [(h, p) for h in range(HALVES) for p in range(pairs)]
    n = len(items)

    def partials(k, dep):
        h, p = items[k]
        parts = []
        for q in range(2):
            lo = (2 * p + q) * width
            x = xs[h] if dep is None else after(xs[h], dep)
            part = jnp.dot(x, weight[:, lo : lo + width], preferred_element_type=jnp.float32)
            part = part.astype(jnp.bfloat16)
            dep = part
            parts.append(part.reshape((2, 2, -1, width)))
        return parts

    activated = [None] * n
    g = [None] * n
    full = [None] * n
    came = [None] * n
    parts = [None] * n
    parts[0] = partials(0, None)
    parts[1] = partials(1, parts[0][1])
    sent = None
    for k in range(n):
        h, p = items[k]
        state = []
        for q in range(2):
            state.append(half_exchange(parts[k][q], by, bx, q == 0, sent))
        sent = state[1][3]
        pre = jnp.concatenate(
            [last_exchange(*state[q], q == 0) for q in range(2)], axis=1
        )
        lo = 2 * p * width
        cot = og[:, h, :, lo : lo + 2 * width].reshape(pre.shape)
        activated[k], g[k] = gelu_pair(pre, cot)
        full[k], came[k] = gather_rows(g[k])
        if k + 2 < n:
            parts[k + 2] = partials(k + 2, g[k])

    def pieces(h):
        x = after(xs[h], g[min(1, n - 1)])
        x = by_distance(x.reshape((2, 2, -1, d_in)), by, bx)
        return x.reshape((-1, d_in)).T

    xts = [pieces(h) for h in range(HALVES)]
    dest = [None]

    def weight_piece(p, q, dep):
        gs = [full[h * pairs + p] for h in range(HALVES)]
        gs[-1] = after(gs[-1], dep)
        dest[0] = weight_grad_columns(xts, gs, p, q, width, (d_in, hidden), dest[0])

    def input_term(k, dep):
        h, p = items[k]
        lo = 2 * p * width
        a = full[k] if dep is None else after(full[k], dep)
        return lax.dot_general(
            a,
            weight[:, lo : lo + 2 * width],
            (((1,), (1,)), ((), ())),
            preferred_element_type=jnp.float32,
        )

    sums = []
    nothing = lambda dep: None
    for h in range(HALVES):
        last = h == HALVES - 1
        total = None
        for p in range(pairs):
            k = h * pairs + p
            if last and p < pairs - 1:
                weight_piece(p, 0, g[n - 1])
                weight_piece(p, 1, came[n - 1])
            dep = g[k + 1] if k + 1 < n else None
            term = input_term(k, dep)
            total = term if total is None else total + term
        works = (nothing, nothing)
        if last:
            works = tuple(functools.partial(weight_piece, pairs - 1, q) for q in range(2))
        sums.append(scatter_sum(total, cols, depths, by, bx, *works).astype(jnp.bfloat16))
    act = jnp.stack(
        [
            jnp.concatenate(activated[h * pairs : (h + 1) * pairs], axis=1).reshape(
                (per_row, m, hidden)
            )
            for h in range(HALVES)
        ],
        axis=1,
    ).reshape((own_rows, hidden))
    return (act, jnp.concatenate(sums, axis=0), dest[0])


def solution(mesh):
    return jax.shard_map(
        functools.partial(body, cols=mesh.shape["col"], depths=mesh.shape["depth"]),
        mesh=mesh,
        in_specs=(
            P(("col", "depth"), "row"),
            P("row", ("col", "depth")),
            P("row", ("col", "depth")),
        ),
        out_specs=(
            P("row", ("col", "depth")),
            P(("col", "depth"), "row"),
            P("row", ("col", "depth")),
        ),
        check_vma=False,
    )
```

```python
import functools
import math

import jax
import jax.numpy as jnp
from jax import lax
from jax.experimental import pallas as pl
from jax.experimental.pallas import tpu as pltpu
from jax.sharding import PartitionSpec as P

gelu_coef = 0.044715
HALVES = 2


def gelu_pair(pre, cotangent):
    scale = math.sqrt(2.0 / math.pi)
    inner = scale * (pre + gelu_coef * pre * pre * pre)
    tanh_val = jnp.tanh(inner)
    activated = (0.5 * pre * (1.0 + tanh_val)).astype(jnp.bfloat16)
    slope = 0.5 * (1.0 + tanh_val) + 0.5 * pre * (1.0 - tanh_val * tanh_val) * scale * (
        1.0 + 3.0 * gelu_coef * pre * pre
    )
    pre_grad = (cotangent.astype(jnp.float32) * slope).astype(jnp.bfloat16)
    return (activated, pre_grad)


def weight_grad_kernel(*refs):
    out_ref = refs[-1]
    xs = refs[:HALVES]
    gs = refs[HALVES : 2 * HALVES]
    total = jnp.dot(xs[0][...], gs[0][...], preferred_element_type=jnp.float32)
    for x, g in zip(xs[1:], gs[1:]):
        total += jnp.dot(x[...], g[...], preferred_element_type=jnp.float32)
    out_ref[...] = total.astype(out_ref.dtype)


def weight_grad_columns(xts, gs, pair, half, width, full_shape, dest):
    rows = full_shape[0]
    depth = gs[0].shape[0]
    bm = 512
    in_specs = [pl.BlockSpec((bm, depth), lambda i: (i, 0)) for _ in xts]
    in_specs += [pl.BlockSpec((depth, width), lambda i: (0, half)) for _ in gs]
    operands = list(xts) + list(gs)
    aliases = {}
    if dest is not None:
        aliases = {len(operands): 0}
        operands.append(dest)
        in_specs.append(pl.BlockSpec(memory_space=pl.ANY))
    flops = 2 * rows * width * depth * len(xts)
    return pl.pallas_call(
        weight_grad_kernel,
        out_shape=jax.ShapeDtypeStruct(full_shape, jnp.bfloat16),
        grid=(rows // bm,),
        in_specs=in_specs,
        out_specs=pl.BlockSpec((bm, width), lambda i: (i, 2 * pair + half)),
        input_output_aliases=aliases,
        compiler_params=pltpu.CompilerParams(vmem_limit_bytes=40 * 1024 * 1024),
        cost_estimate=pl.CostEstimate(
            flops=flops, bytes_accessed=2 * rows * width + 4 * rows * depth, transcendentals=0
        ),
    )(*operands)


def swap(x, flip):
    return lax.ppermute(x, "row", [(i, i ^ flip) for i in range(4)])


def pick(x, axis, index):
    return lax.dynamic_index_in_dim(x, index, axis, keepdims=False)


def after(x, *deps):
    return lax.optimization_barrier((x,) + deps)[0]


def by_distance(x, by, bx):
    x = jnp.where(by == 0, x, x[::-1])
    return jnp.where(bx == 0, x, x[:, ::-1])


def laid(shape, blocks):
    out = jnp.zeros(shape, jnp.bfloat16)
    for block, place in blocks:
        out = lax.dynamic_update_slice(out, block, place)
    return out


def half_exchange(part, by, bx, x_first, dep):
    if dep is not None:
        part = after(part, dep)
    if x_first:
        got = swap(pick(part, 1, 1 - bx), 1)
        kept, bit = pick(part, 1, bx), by
    else:
        got = swap(pick(part, 0, 1 - by), 2)
        kept, bit = pick(part, 0, by), bx
    send = pick(kept, 0, 1 - bit).astype(jnp.float32) + pick(got, 0, 1 - bit).astype(jnp.float32)
    return kept, got, bit, send.astype(jnp.bfloat16)


def last_exchange(kept, got, bit, send, x_first):
    last = swap(send, 2 if x_first else 1)
    own = pick(kept, 0, bit).astype(jnp.float32) + pick(got, 0, bit).astype(jnp.float32)
    return own + last.astype(jnp.float32)


def gather_rows(g):
    over_y = swap(g, 2)
    over_x = swap(g, 1)
    cut = g.shape[1] // 2
    low, high = swap(over_y[:, :cut], 1), swap(over_x[:, cut:], 2)
    m = g.shape[0]
    places = [(g, (0, 0)), (over_x, (m, 0)), (over_y, (2 * m, 0))]
    places += [(low, (3 * m, 0)), (high, (3 * m, cut))]
    return laid((4 * m, g.shape[1]), places), over_y


def scatter_sum(part, cols, depths, by, bx, first_work, second_work):
    width = part.shape[1]
    if cols != 2 or depths != 4:
        flat = by_distance(part.reshape((2, 2, -1, width)), by, bx).reshape((-1, width))
        out = lax.psum_scatter(flat, ("col", "depth"), scatter_dimension=0, tiled=True)
        first_work(part)
        second_work(part)
        return out, [part] * 3
    part = part.reshape((2, 2 * 2, -1, width))
    me_c, me_d = lax.axis_index("col"), lax.axis_index("depth")
    send = pick(part, 0, (1 - me_c) ^ by).astype(jnp.bfloat16)
    got = lax.ppermute(send, "col", [(0, 1), (1, 0)])
    kept = pick(part, 0, me_c ^ by) + got.astype(jnp.float32)

    def block(d):
        return pick(kept, 0, ((d // 2) ^ bx) * 2 + d % 2)

    ring = [(i, (i + 1) % depths) for i in range(depths)]
    acc = block((me_d + depths - 1) % depths)
    outs = []
    for step in range(depths - 1):
        out = acc.astype(jnp.bfloat16)
        outs.append(out)
        got = lax.ppermute(out, "depth", ring)
        if step == 0:
            first_work(out)
        if step == 1:
            second_work(out)
        acc = got.astype(jnp.float32) + block((me_d + 2 * depths - 2 - step) % depths)
    return acc, outs


def body(inputs, weight, out_grad, *, cols, depths):
    tok, d_in = inputs.shape
    own_rows, hidden = out_grad.shape
    m = tok // HALVES
    per_row = own_rows // tok
    pairs = 2 if hidden % 1024 == 0 and hidden >= 2048 else 1
    width = hidden // (2 * pairs)
    row = lax.axis_index("row")
    by, bx = row // 2, row % 2

    xs = [
        lax.all_gather(inputs[h * m : (h + 1) * m], ("col", "depth"), axis=0, tiled=True)
        for h in range(HALVES)
    ]
    og = out_grad.reshape((per_row, HALVES, m, hidden))
    items = [(h, p) for h in range(HALVES) for p in range(pairs)]
    n = len(items)

    def partials(k, dep):
        h, p = items[k]
        parts = []
        for q in range(2):
            lo = (2 * p + q) * width
            x = xs[h] if dep is None else after(xs[h], dep)
            part = jnp.dot(x, weight[:, lo : lo + width], preferred_element_type=jnp.float32)
            part = part.astype(jnp.bfloat16)
            dep = part
            parts.append(part.reshape((2, 2, -1, width)))
        return parts

    activated = [None] * n
    g = [None] * n
    full = [None] * n
    came = [None] * n
    parts = [None] * n
    parts[0] = partials(0, None)
    parts[1] = partials(1, parts[0][1])
    sent = None
    for k in range(n):
        h, p = items[k]
        state = []
        for q in range(2):
            state.append(half_exchange(parts[k][q], by, bx, q == 0, sent))
        sent = state[1][3]
        pre = jnp.concatenate(
            [last_exchange(*state[q], q == 0) for q in range(2)], axis=1
        )
        lo = 2 * p * width
        cot = og[:, h, :, lo : lo + 2 * width].reshape(pre.shape)
        activated[k], g[k] = gelu_pair(pre, cot)
        full[k], came[k] = gather_rows(g[k])
        if k + 2 < n:
            parts[k + 2] = partials(k + 2, g[k])

    def pieces(h):
        x = after(xs[h], g[min(1, n - 1)])
        x = x.reshape((4, -1, d_in))
        size = x.shape[1]
        blocks = [(pick(x, 0, row ^ k), (k * size, 0)) for k in range(4)]
        return laid((4 * size, d_in), blocks).T

    xts = [pieces(h) for h in range(HALVES)]
    dest = [None]

    def weight_piece(p, q, dep):
        gs = [full[h * pairs + p] for h in range(HALVES)]
        gs[-1] = after(gs[-1], dep)
        dest[0] = weight_grad_columns(xts, gs, p, q, width, (d_in, hidden), dest[0])

    def input_term(k, dep):
        h, p = items[k]
        lo = 2 * p * width
        a = full[k] if dep is None else after(full[k], dep)
        return lax.dot_general(
            a,
            weight[:, lo : lo + 2 * width],
            (((1,), (1,)), ((), ())),
            preferred_element_type=jnp.float32,
        )

    sums = []
    nothing = lambda dep: None
    for h in range(HALVES):
        last = h == HALVES - 1
        total = None
        for p in range(pairs):
            k = h * pairs + p
            if last and p < pairs - 1:
                weight_piece(p, 0, outs[1])
                weight_piece(p, 1, outs[2])
            dep = g[k + 1] if k + 1 < n else None
            if last and p < pairs - 1:
                dep = outs[0]
            term = input_term(k, dep)
            total = term if total is None else total + term
        works = (nothing, nothing)
        if last:
            works = tuple(functools.partial(weight_piece, pairs - 1, q) for q in range(2))
        total, outs = scatter_sum(total, cols, depths, by, bx, *works)
        sums.append(total.astype(jnp.bfloat16))
    act = jnp.stack(
        [
            jnp.concatenate(activated[h * pairs : (h + 1) * pairs], axis=1).reshape(
                (per_row, m, hidden)
            )
            for h in range(HALVES)
        ],
        axis=1,
    ).reshape((own_rows, hidden))
    return (act, jnp.concatenate(sums, axis=0), dest[0])


def solution(mesh):
    return jax.shard_map(
        functools.partial(body, cols=mesh.shape["col"], depths=mesh.shape["depth"]),
        mesh=mesh,
        in_specs=(
            P(("col", "depth"), "row"),
            P("row", ("col", "depth")),
            P("row", ("col", "depth")),
        ),
        out_specs=(
            P("row", ("col", "depth")),
            P(("col", "depth"), "row"),
            P("row", ("col", "depth")),
        ),
        check_vma=False,
    )
```
